512 devices in a mesh: dp: 64 (over x, z), et: 8 (over y, core).
Axes of the slice: x: 4, y: 4, z: 16, core: 2. Of those that a mesh axis runs over, the one named last changes fastest.
Arguments:
- token_rows: bfloat16 [16384, 3072], P(('dp', 'et')), may hold values from -6 to 6
- route_weight: float32 [16384], P(('dp', 'et')), may hold values from 0.05 to 1
- live_count: int32 [512], P(('dp', 'et')), may hold values from 1 to 32, as said below
- gate_pre: bfloat16 [16384, 8192], P('dp', 'et'), may hold values from -10 to 10
- up_pre: bfloat16 [16384, 8192], P('dp', 'et'), may hold values from -6 to 6
- hidden_grad: bfloat16 [16384, 8192], P('dp', 'et'), may hold values from -6 to 6
Outputs:
- gate_grad: float32 [3072, 8192], P('dp', 'et')
The draws below stay inside these ranges and needn't reach their ends.
Inputs may be any that keep to these rules, and one draw needn't show every extreme that they name: The first live_count slots of each device are live. Some device has exactly 32 and some exactly 1.
All inputs are finite; a program needn't handle non-finite values.
Results may differ from the reference program's by a relative error of at most 0.004.
Values may be sent and summed in bfloat16 or wider, within the bound.
No kernel may reach another device: no remote copies, remote signals or barrier semaphores. Data moves between devices by JAX's collectives and lax.ppermute only.
A program may use at most 128 MiB of HBM per device.

```python
import math
import jax
import jax.numpy as jnp
from jax import lax

D = 3072
TOK_DEV = 32
FF = 8192
TOKENS = 16384
N_ET = 8


def draw_live_count(key, part):
    key = jax.random.fold_in(key, 11)
    key_base, key_top, key_low = jax.random.split(key, 3)
    device_count = TOKENS // TOK_DEV
    counts = jax.random.randint(key_base, (device_count,), 1, TOK_DEV + 1)
    top_index = jax.random.randint(key_top, (), 0, device_count)
    low_index = (top_index + 1 + jax.random.randint(key_low, (), 0, device_count - 1)) % device_count
    counts = counts.at[top_index].set(TOK_DEV)
    counts = counts.at[low_index].set(1)
    return counts.astype(jnp.int32)


def level_of(rng, shape, pieces, smallest, top_value):
    factor_of, own = 1.0, jax.random.fold_in(rng, 6)
    for axis_at, parts in pieces:
        heights = jnp.exp(jax.random.uniform(jax.random.fold_in(own, axis_at), (parts,), jnp.float32, smallest / len(pieces), top_value / len(pieces)))
        factor_of = factor_of * jnp.repeat(heights, shape[axis_at] // parts).reshape([-1 if axis == axis_at else 1 for axis in range(len(shape))])
    return factor_of


def gaussian(stream_key, shape, width, most, cuts=(), kind=jnp.bfloat16):
    drawn = width * jax.random.normal(stream_key, shape, jnp.float32)
    if cuts:
        drawn = drawn * level_of(stream_key, shape, cuts, -0.22, 0.18)
    return jnp.clip(drawn, -most, most).astype(kind)


def setup_inputs(seed: int = 0) -> dict:
    key_list = jax.random.split(jax.random.key(seed), 7)
    token_rows = gaussian(key_list[0], (TOKENS, D), 1.0, 6.0, ((0, 512),))
    route_weight = jnp.clip(0.05 + 0.95 * jax.random.uniform(key_list[1], (TOKENS,), jnp.float32) ** level_of(key_list[1], (TOKENS,), ((0, 512),), -0.2, 0.2), 0.05, 1.0)
    live_count = draw_live_count(jax.random.fold_in(key_list[6], 71), 0)
    gate_pre = gaussian(key_list[3], (TOKENS, FF), 2.0, 10.0, ((0, 64), (1, 8)))
    up_pre = gaussian(key_list[4], (TOKENS, FF), 1.0, 6.0, ((0, 64), (1, 8)))
    hidden_grad = gaussian(key_list[5], (TOKENS, FF), 1.0, 6.0, ((0, 64), (1, 8)))
    return {"token_rows": token_rows, "route_weight": route_weight, "live_count": live_count, "gate_pre": gate_pre, "up_pre": up_pre, "hidden_grad": hidden_grad}


def gate_slope(gate_pre, up_pre, hidden_grad):
    gate_value = gate_pre.astype(jnp.float32)
    sigmoid_v = jax.nn.sigmoid(gate_value)
    silu_slope = sigmoid_v * (1.0 + gate_value * (1.0 - sigmoid_v))
    return (hidden_grad.astype(jnp.float32) * up_pre.astype(jnp.float32) * silu_slope).astype(jnp.bfloat16)

def reference(token_rows, route_weight, live_count, gate_pre, up_pre, hidden_grad):
    device_count = live_count.shape[0]
    row_count = token_rows.shape[0] // device_count
    live_rows = (jnp.arange(row_count, dtype=jnp.int32)[None, :] < live_count[:, None]).reshape(-1)
    factor_rows = route_weight.astype(jnp.float32) * live_rows.astype(jnp.float32)
    weighted = (token_rows.astype(jnp.float32) * factor_rows[:, None]).astype(jnp.bfloat16)
    group_rows = TOK_DEV * N_ET
    step_count = token_rows.shape[0] // group_rows
    weighted_blocks = weighted.reshape(step_count, group_rows, D)
    gate_blocks = gate_pre.reshape(step_count, group_rows, FF)
    up_blocks = up_pre.reshape(step_count, group_rows, FF)
    grad_blocks = hidden_grad.reshape(step_count, group_rows, FF)

    def accumulate(running, items):
        row_block, gate_block, up_block, grad_block = items
        gate_delta = gate_slope(gate_block, up_block, grad_block)
        return (running + jnp.dot(row_block.T, gate_delta, preferred_element_type=jnp.float32), None)
    running, unused = lax.scan(accumulate, jnp.zeros((D, FF), jnp.float32), (weighted_blocks, gate_blocks, up_blocks, grad_blocks))
    return running * (1.0 / math.sqrt(TOKENS))
```

```python
import math

import jax
import jax.numpy as jnp
from jax import lax
from jax.sharding import Mesh, PartitionSpec as P

X, ZH, ZL, Y, C = 4, 4, 4, 4, 2
Z = ("zh", "zl")
DP = ("x", "zh", "zl")
ET = ("y", "c")


def gate_slope(gate_pre, up_pre, hidden_grad):
    gate_value = gate_pre.astype(jnp.float32)
    sigmoid_v = jax.nn.sigmoid(gate_value)
    silu_slope = sigmoid_v * (1.0 + gate_value * (1.0 - sigmoid_v))
    return (hidden_grad.astype(jnp.float32) * up_pre.astype(jnp.float32) * silu_slope).astype(
        jnp.bfloat16
    )


def z_shift(value, step):
    return lax.ppermute(value, Z, [(i, (i + step) % (ZH * ZL)) for i in range(ZH * ZL)])


def pick(value, index, axis):
    return lax.dynamic_index_in_dim(value, index, axis, keepdims=False)


def f32(value):
    return value.astype(jnp.float32)


def shards(token_rows, route_weight, live_count, gate_pre, up_pre, hidden_grad):
    rows, features = token_rows.shape
    units = gate_pre.shape[1]
    part = features // X
    owned = part // (ZH * ZL)
    core = lax.axis_index("c")
    zl = lax.axis_index("zl")

    delta = gate_slope(gate_pre, up_pre, hidden_grad).reshape(Y, C, rows, units)
    delta = jnp.stack([pick(delta, core, 1), pick(delta, 1 - core, 1)])
    delta = lax.all_gather(delta.reshape(C * Y * rows, units), "x", axis=0, tiled=False)

    live_rows = jnp.arange(rows, dtype=jnp.int32) < live_count[0]
    factor_rows = route_weight * live_rows.astype(jnp.float32)
    weighted = (f32(token_rows) * factor_rows[:, None]).astype(jnp.bfloat16)
    parts = weighted.reshape(rows, X, part).transpose(1, 0, 2)
    parts = jnp.broadcast_to(parts[:, None], (X, Y, rows, part)).reshape(X * Y, rows, part)
    own = lax.all_to_all(parts, ("x", "y"), 0, 0)
    other = lax.ppermute(own, "c", [(0, 1), (1, 0)])
    tokens = jnp.stack(
        [own.reshape(X, Y * rows, part), other.reshape(X, Y * rows, part)], axis=1
    )

    product = lax.dot_general(
        tokens.reshape(X * C * Y * rows, part),
        delta.reshape(X * C * Y * rows, units),
        (((0,), (0,)), ((), ())),
        preferred_element_type=jnp.float32,
    ).reshape(ZH, ZL, owned, units)

    half = units // 2
    above = pick(product, (zl + 1) % ZL, 1).astype(jnp.bfloat16)
    below = pick(product, (zl + 3) % ZL, 1).astype(jnp.bfloat16)
    across = pick(product, (zl + 2) % ZL, 1).astype(jnp.bfloat16)
    total = pick(product, zl, 1)
    far = jnp.concatenate(
        [f32(z_shift(across[..., :half], -2)), f32(z_shift(across[..., half:], 2))], axis=-1
    )
    total = total + f32(z_shift(above, 1)) + f32(z_shift(below, -1)) + far

    arrived = lax.all_to_all(total.astype(jnp.bfloat16), "zh", 0, 0)
    count = rows * X * ZH * ZL * Y * C
    return f32(arrived).sum(0) * (1.0 / math.sqrt(count))


def solution(mesh):
    fine = Mesh(mesh.devices.reshape(X, ZH, ZL, Y, C), ("x", "zh", "zl", "y", "c"))
    placed = (P(DP + ET, None), P(DP + ET), P(DP + ET), P(DP, ET), P(DP, ET), P(DP, ET))
    return jax.shard_map(
        shards, mesh=fine, in_specs=placed, out_specs=P(DP, ET), check_vma=False
    )
```

```python
import functools
import math

import jax
import jax.numpy as jnp
from jax import lax
from jax.experimental import pallas as pl
from jax.experimental.pallas import tpu as pltpu
from jax.sharding import Mesh, PartitionSpec as P

X, Z, Y, C = 4, 16, 4, 2
W = 4
DP = ("x", "z")
ET = ("y", "c")
VMEM = pl.BlockSpec(memory_space=pltpu.VMEM)
SMEM = pl.BlockSpec(memory_space=pltpu.SMEM)
PARAMS = pltpu.CompilerParams(vmem_limit_bytes=11 * 512 * 1024)


def f32(value):
    return value.astype(jnp.float32)


def bf16(value):
    return value.astype(jnp.bfloat16)


def x_shift(value, step):
    return lax.ppermute(value, "x", [(i, (i + step) % X) for i in range(X)])


def x_forward(value):
    pairs = [(x * C + c, (x + 1 - 2 * c) % X * C + c) for x in range(X) for c in range(C)]
    return lax.ppermute(value, ("x", "c"), pairs)


def z_shift(value, step):
    return lax.ppermute(value, "z", [(i, (i + step) % Z) for i in range(Z)])


def z_apart(value, step):
    pairs = [(z * C + c, (z - step + 2 * step * c) % Z * C + c) for z in range(Z) for c in range(C)]
    return lax.ppermute(value, ("z", "c"), pairs)


def delta_kernel(at, gate_ref, up_ref, grad_ref, out_ref):
    rows = gate_ref.shape[2]
    for place in range(C):
        source = (at[0] + place) % C
        for y in range(Y):
            gate = f32(gate_ref[y, source])
            sigmoid_v = jax.nn.sigmoid(gate)
            slope = sigmoid_v * (1.0 + gate * (1.0 - sigmoid_v))
            value = f32(grad_ref[y, source]) * f32(up_ref[y, source]) * slope
            out_ref[(place * Y + y) * rows : (place * Y + y + 1) * rows, :] = bf16(value)


def slab_kernel(at, total_ref, keep_ref, *sent_refs):
    for j in range(Z // W):
        keep_ref[j] = total_ref[j * W + at[0]]
        for step, sent_ref in enumerate(sent_refs):
            sent_ref[j] = bf16(total_ref[j * W + (at[0] + step + 1) % W])


def window_kernel(at, keep_ref, far_ref, above_ref, below_ref, own_ref, *sent_refs):
    for step, out_ref in enumerate((own_ref,) + sent_refs):
        j = (at[0] + step) % (Z // W)
        value = keep_ref[j] + f32(far_ref[j]) + f32(above_ref[j]) + f32(below_ref[j])
        out_ref[...] = value.astype(out_ref.dtype)


def shards(token_rows, route_weight, live_count, gate_pre, up_pre, hidden_grad):
    rows, features = token_rows.shape
    units = gate_pre.shape[1]
    part = features // X
    owned = part // Z
    core = lax.axis_index("c")
    x_at = lax.axis_index("x")
    z_at = lax.axis_index("z")
    shape = jax.ShapeDtypeStruct

    live_rows = jnp.arange(rows, dtype=jnp.int32) < live_count[0]
    factor = route_weight * f32(live_rows)
    weighted = bf16(f32(token_rows) * factor[:, None])
    weighted = jnp.broadcast_to(weighted[None], (Y, rows, features))
    by_core = [value.reshape(Y, C, rows, units) for value in (gate_pre, up_pre, hidden_grad)]
    tall = Y * C * rows
    chunk = 256
    piece = pl.BlockSpec((Y, C, rows, chunk), lambda n, at: (0, 0, 0, n))
    delta = pl.pallas_call(
        delta_kernel,
        out_shape=shape((tall, units), jnp.bfloat16),
        grid_spec=pltpu.PrefetchScalarGridSpec(
            num_scalar_prefetch=1,
            grid=(units // chunk,),
            in_specs=[piece] * 3,
            out_specs=pl.BlockSpec((tall, chunk), lambda n, at: (0, n)),
        ),
        compiler_params=PARAMS,
        name="gate_delta",
    )(jnp.stack([core]), *by_core)

    along_y = lax.all_to_all(weighted, "y", 0, 0)
    parts = along_y.reshape(Y * rows, X, part).transpose(1, 0, 2)
    before, after = x_shift(delta, 1), x_shift(delta, -1)
    across = x_forward(jnp.where(core == 0, before, after))
    own = lax.all_to_all(parts, "x", 0, 0)
    own = jnp.stack(
        [
            lax.dynamic_index_in_dim(own, (x_at + step) % X, 0, keepdims=False)
            for step in (0, X - 1, 1, 2)
        ]
    )
    own, across = lax.optimization_barrier((own, across))
    other = lax.ppermute(own, "c", [(0, 1), (1, 0)])
    product = 0.0
    for place, tokens in enumerate((own, other)):
        span = slice(place * Y * rows, (place + 1) * Y * rows)
        right = jnp.concatenate([block[span] for block in (delta, before, after, across)], axis=0)
        product += lax.dot_general(
            tokens.reshape(X * Y * rows, part),
            right,
            (((0,), (0,)), ((), ())),
            preferred_element_type=jnp.float32,
        )

    count = Z // W
    keep, above, across_rows, below = pl.pallas_call(
        slab_kernel,
        out_shape=[shape((count, owned, units), jnp.float32)]
        + [shape((count, owned, units), jnp.bfloat16)] * (W - 1),
        in_specs=[SMEM, VMEM],
        out_specs=[VMEM] * W,
        compiler_params=PARAMS,
        name="slabs",
    )(jnp.stack([z_at % W]), product.reshape(Z, owned, units))

    far = z_apart(across_rows, 2)
    above = z_shift(above, 1)
    below = z_shift(below, -1)
    own_block, *blocks = pl.pallas_call(
        window_kernel,
        out_shape=[shape((owned, units), jnp.float32)]
        + [shape((owned, units), jnp.bfloat16)] * (count - 1),
        in_specs=[SMEM] + [VMEM] * 4,
        out_specs=[VMEM] * count,
        compiler_params=PARAMS,
        name="window",
    )(jnp.stack([z_at // W]), keep, far, above, below)

    total = own_block
    for step in (2, 1, 3):
        total += f32(z_shift(blocks[step - 1], W * step))
    return total * (1.0 / math.sqrt(rows * X * Z * Y * C))


def solution(mesh):
    fine = Mesh(mesh.devices.reshape(X, Z, Y, C), ("x", "z", "y", "c"))
    placed = (P(DP + ET, None), P(DP + ET), P(DP + ET), P(DP, ET), P(DP, ET), P(DP, ET))
    return jax.shard_map(
        shards, mesh=fine, in_specs=placed, out_specs=P(DP, ET), check_vma=False
    )
```

```python
import functools
import math

import jax
import jax.numpy as jnp
from jax import lax
from jax.experimental import pallas as pl
from jax.experimental.pallas import tpu as pltpu
from jax.sharding import Mesh, PartitionSpec as P

X, Z, Y, C = 4, 16, 4, 2
W = 4
DP = ("x", "z")
ET = ("y", "c")
VMEM = pl.BlockSpec(memory_space=pltpu.VMEM)
SMEM = pl.BlockSpec(memory_space=pltpu.SMEM)
PARAMS = pltpu.CompilerParams(vmem_limit_bytes=11 * 512 * 1024)


def f32(value):
    return value.astype(jnp.float32)


def bf16(value):
    return value.astype(jnp.bfloat16)


def x_shift(value, step):
    return lax.ppermute(value, "x", [(i, (i + step) % X) for i in range(X)])


def x_forward(value):
    pairs = [(x * C + c, (x + 1 - 2 * c) % X * C + c) for x in range(X) for c in range(C)]
    return lax.ppermute(value, ("x", "c"), pairs)


def z_shift(value, step):
    return lax.ppermute(value, "z", [(i, (i + step) % Z) for i in range(Z)])


def z_apart(value, step):
    pairs = [(z * C + c, (z - step + 2 * step * c) % Z * C + c) for z in range(Z) for c in range(C)]
    return lax.ppermute(value, ("z", "c"), pairs)


def delta_kernel(at, gate_ref, up_ref, grad_ref, out_ref):
    rows = gate_ref.shape[2]
    for place in range(C):
        source = (at[0] + place) % C
        for y in range(Y):
            gate = f32(gate_ref[y, source])
            sigmoid_v = jax.nn.sigmoid(gate)
            slope = sigmoid_v * (1.0 + gate * (1.0 - sigmoid_v))
            value = f32(grad_ref[y, source]) * f32(up_ref[y, source]) * slope
            out_ref[(place * Y + y) * rows : (place * Y + y + 1) * rows, :] = bf16(value)


def spread_kernel(rows_ref, out_ref):
    for place in range(Y):
        out_ref[place] = rows_ref[...]


def choose_kernel(at, before_ref, after_ref, out_ref):
    @pl.when(at[0] == 0)
    def _():
        out_ref[...] = before_ref[...]

    @pl.when(at[0] != 0)
    def _():
        out_ref[...] = after_ref[...]


def order_kernel(at, rows_ref, out_ref):
    rows = rows_ref.shape[2]
    for place in range(X):
        for y in range(Y):
            start = (place * Y + y) * rows
            out_ref[start : start + rows, :] = rows_ref[y, at[place]]


def slab_kernel(at, total_ref, keep_ref, *sent_refs):
    for j in range(Z // W):
        keep_ref[j] = total_ref[j * W + at[0]]
        for step, sent_ref in enumerate(sent_refs):
            sent_ref[j] = bf16(total_ref[j * W + (at[0] + step + 1) % W])


def window_kernel(at, keep_ref, far_ref, above_ref, below_ref, own_ref, *sent_refs):
    for step, out_ref in enumerate((own_ref,) + sent_refs):
        j = (at[0] + step) % (Z // W)
        value = keep_ref[j] + f32(far_ref[j]) + f32(above_ref[j]) + f32(below_ref[j])
        out_ref[...] = value.astype(out_ref.dtype)


def shards(token_rows, route_weight, live_count, gate_pre, up_pre, hidden_grad):
    rows, features = token_rows.shape
    units = gate_pre.shape[1]
    part = features // X
    owned = part // Z
    core = lax.axis_index("c")
    x_at = lax.axis_index("x")
    z_at = lax.axis_index("z")
    shape = jax.ShapeDtypeStruct

    live_rows = jnp.arange(rows, dtype=jnp.int32) < live_count[0]
    factor = route_weight * f32(live_rows)
    weighted = bf16(f32(token_rows) * factor[:, None])
    by_core = [value.reshape(Y, C, rows, units) for value in (gate_pre, up_pre, hidden_grad)]
    tall = Y * C * rows
    chunk = 256
    piece = pl.BlockSpec((Y, C, rows, chunk), lambda n, at: (0, 0, 0, n))
    delta = pl.pallas_call(
        delta_kernel,
        out_shape=shape((tall, units), jnp.bfloat16),
        grid_spec=pltpu.PrefetchScalarGridSpec(
            num_scalar_prefetch=1,
            grid=(units // chunk,),
            in_specs=[piece] * 3,
            out_specs=pl.BlockSpec((tall, chunk), lambda n, at: (0, n)),
        ),
        compiler_params=PARAMS,
        name="gate_delta",
    )(jnp.stack([core]), *by_core)

    half = Y * rows
    parts = lax.all_to_all(weighted.reshape(rows, X, part).transpose(1, 0, 2), "x", 0, 0)
    parts, delta = lax.optimization_barrier((parts, delta))
    before, after = x_shift(delta, 1), x_shift(delta, -1)
    chosen = pl.pallas_call(
        choose_kernel,
        out_shape=shape(delta.shape, delta.dtype),
        in_specs=[SMEM, VMEM, VMEM],
        out_specs=VMEM,
        compiler_params=PARAMS,
        cost_estimate=pl.CostEstimate(flops=int(2.3e+10), bytes_accessed=0, transcendentals=0),
        name="chosen",
    )(jnp.stack([core]), before, after)
    across = x_forward(chosen)
    spread = pl.pallas_call(
        spread_kernel,
        out_shape=shape((Y, X, rows, part), jnp.bfloat16),
        in_specs=[VMEM],
        out_specs=VMEM,
        compiler_params=PARAMS,
        cost_estimate=pl.CostEstimate(flops=int(2.3e+10), bytes_accessed=0, transcendentals=0),
        name="spread",
    )(parts)
    own = lax.all_to_all(spread, "y", 0, 0)

    own = pl.pallas_call(
        order_kernel,
        out_shape=shape((X * half, part), jnp.bfloat16),
        in_specs=[SMEM, VMEM],
        out_specs=VMEM,
        compiler_params=PARAMS,
        cost_estimate=pl.CostEstimate(flops=int(2.3e+10), bytes_accessed=0, transcendentals=0),
        name="ordered_rows",
    )((x_at + jnp.array([0, X - 1, 1, 2])) % X, own)
    other = lax.ppermute(own, "c", [(0, 1), (1, 0)])
    product = 0.0
    for place, tokens in enumerate((own, other)):
        span = slice(place * half, (place + 1) * half)
        right = [block[span] for block in (delta, before, after, across)]
        product += lax.dot_general(
            tokens,
            jnp.concatenate(right, axis=0),
            (((0,), (0,)), ((), ())),
            preferred_element_type=jnp.float32,
        )

    count = Z // W
    keep, above, across_rows, below = pl.pallas_call(
        slab_kernel,
        out_shape=[shape((count, owned, units), jnp.float32)]
        + [shape((count, owned, units), jnp.bfloat16)] * (W - 1),
        in_specs=[SMEM, VMEM],
        out_specs=[VMEM] * W,
        compiler_params=PARAMS,
        name="slabs",
    )(jnp.stack([z_at % W]), product.reshape(Z, owned, units))

    far = z_apart(across_rows, 2)
    above = z_shift(above, 1)
    below = z_shift(below, -1)
    own_block, *blocks = pl.pallas_call(
        window_kernel,
        out_shape=[shape((owned, units), jnp.float32)]
        + [shape((owned, units), jnp.bfloat16)] * (count - 1),
        in_specs=[SMEM] + [VMEM] * 4,
        out_specs=[VMEM] * count,
        compiler_params=PARAMS,
        name="window",
    )(jnp.stack([z_at // W]), keep, far, above, below)

    total = own_block
    for step in (2, 1, 3):
        total += f32(z_shift(blocks[step - 1], W * step))
    return total * (1.0 / math.sqrt(rows * X * Z * Y * C))


def solution(mesh):
    fine = Mesh(mesh.devices.reshape(X, Z, Y, C), ("x", "z", "y", "c"))
    placed = (P(DP + ET, None), P(DP + ET), P(DP + ET), P(DP, ET), P(DP, ET), P(DP, ET))
    return jax.shard_map(
        shards, mesh=fine, in_specs=placed, out_specs=P(DP, ET), check_vma=False
    )
```

```python
import functools
import math

import jax
import jax.numpy as jnp
from jax import lax
from jax.experimental import pallas as pl
from jax.experimental.pallas import tpu as pltpu
from jax.sharding import Mesh, PartitionSpec as P

X, Z, Y, C = 4, 16, 4, 2
W = 4
DP = ("x", "z")
ET = ("y", "c")
VMEM = pl.BlockSpec(memory_space=pltpu.VMEM)
SMEM = pl.BlockSpec(memory_space=pltpu.SMEM)
PARAMS = pltpu.CompilerParams(vmem_limit_bytes=11 * 512 * 1024)


def f32(value):
    return value.astype(jnp.float32)


def bf16(value):
    return value.astype(jnp.bfloat16)


def x_shift(value, step):
    return lax.ppermute(value, "x", [(i, (i + step) % X) for i in range(X)])


def x_forward(value):
    pairs = [(x * C + c, (x + 1 - 2 * c) % X * C + c) for x in range(X) for c in range(C)]
    return lax.ppermute(value, ("x", "c"), pairs)


def z_shift(value, step):
    return lax.ppermute(value, "z", [(i, (i + step) % Z) for i in range(Z)])


def z_apart(value, step):
    pairs = [(z * C + c, (z - step + 2 * step * c) % Z * C + c) for z in range(Z) for c in range(C)]
    return lax.ppermute(value, ("z", "c"), pairs)


def delta_kernel(at, gate_ref, up_ref, grad_ref, out_ref):
    rows = gate_ref.shape[2]
    for place in range(C):
        source = (at[0] + place) % C
        for y in range(Y):
            gate = f32(gate_ref[y, source])
            sigmoid_v = jax.nn.sigmoid(gate)
            slope = sigmoid_v * (1.0 + gate * (1.0 - sigmoid_v))
            value = f32(grad_ref[y, source]) * f32(up_ref[y, source]) * slope
            out_ref[(place * Y + y) * rows : (place * Y + y + 1) * rows, :] = bf16(value)


def spread_kernel(rows_ref, out_ref):
    for place in range(Y):
        out_ref[place] = rows_ref[...]


def choose_kernel(at, before_ref, after_ref, out_ref):
    @pl.when(at[0] == 0)
    def _():
        out_ref[...] = before_ref[...]

    @pl.when(at[0] != 0)
    def _():
        out_ref[...] = after_ref[...]


def order_kernel(at, rows_ref, out_ref):
    rows = rows_ref.shape[2]
    for place in range(X):
        for y in range(Y):
            start = (place * Y + y) * rows
            out_ref[start : start + rows, :] = rows_ref[y, at[place]]


def slab_kernel(at, total_ref, keep_ref, *sent_refs):
    for j in range(Z // W):
        keep_ref[j] = total_ref[j * W + at[0]]
        for step, sent_ref in enumerate(sent_refs):
            sent_ref[j] = bf16(total_ref[j * W + (at[0] + step + 1) % W])


def window_kernel(at, keep_ref, far_ref, above_ref, below_ref, own_ref, *sent_refs):
    for step, out_ref in enumerate((own_ref,) + sent_refs):
        j = (at[0] + step) % (Z // W)
        value = keep_ref[j] + f32(far_ref[j]) + f32(above_ref[j]) + f32(below_ref[j])
        out_ref[...] = value.astype(out_ref.dtype)


def shards(token_rows, route_weight, live_count, gate_pre, up_pre, hidden_grad):
    rows, features = token_rows.shape
    units = gate_pre.shape[1]
    part = features // X
    owned = part // Z
    core = lax.axis_index("c")
    x_at = lax.axis_index("x")
    z_at = lax.axis_index("z")
    shape = jax.ShapeDtypeStruct

    live_rows = jnp.arange(rows, dtype=jnp.int32) < live_count[0]
    factor = route_weight * f32(live_rows)
    weighted = bf16(f32(token_rows) * factor[:, None])
    by_core = [value.reshape(Y, C, rows, units) for value in (gate_pre, up_pre, hidden_grad)]
    tall = Y * C * rows
    chunk = 256
    piece = pl.BlockSpec((Y, C, rows, chunk), lambda n, at: (0, 0, 0, n))
    delta = pl.pallas_call(
        delta_kernel,
        out_shape=shape((tall, units), jnp.bfloat16),
        grid_spec=pltpu.PrefetchScalarGridSpec(
            num_scalar_prefetch=1,
            grid=(units // chunk,),
            in_specs=[piece] * 3,
            out_specs=pl.BlockSpec((tall, chunk), lambda n, at: (0, n)),
        ),
        compiler_params=PARAMS,
        name="gate_delta",
    )(jnp.stack([core]), *by_core)

    half = Y * rows
    parts = lax.all_to_all(weighted.reshape(rows, X, part).transpose(1, 0, 2), "x", 0, 0)
    parts, delta = lax.optimization_barrier((parts, delta))
    before, after = x_shift(delta, 1), x_shift(delta, -1)
    chosen = pl.pallas_call(
        choose_kernel,
        out_shape=shape(delta.shape, delta.dtype),
        in_specs=[SMEM, VMEM, VMEM],
        out_specs=VMEM,
        compiler_params=PARAMS,
        cost_estimate=pl.CostEstimate(flops=int(2.3e+10), bytes_accessed=0, transcendentals=0),
        name="chosen",
    )(jnp.stack([core]), before, after)
    across = x_forward(chosen)
    spread = pl.pallas_call(
        spread_kernel,
        out_shape=shape((Y, X, rows, part), jnp.bfloat16),
        in_specs=[VMEM],
        out_specs=VMEM,
        compiler_params=PARAMS,
        cost_estimate=pl.CostEstimate(flops=int(2.3e+10), bytes_accessed=0, transcendentals=0),
        name="spread",
    )(parts)
    own = lax.all_to_all(spread, "y", 0, 0)

    own = pl.pallas_call(
        order_kernel,
        out_shape=shape((X * half, part), jnp.bfloat16),
        in_specs=[SMEM, VMEM],
        out_specs=VMEM,
        compiler_params=PARAMS,
        cost_estimate=pl.CostEstimate(flops=int(2.3e+10), bytes_accessed=0, transcendentals=0),
        name="ordered_rows",
    )((x_at + jnp.array([0, X - 1, 1, 2])) % X, own)
    other = lax.ppermute(own, "c", [(0, 1), (1, 0)])
    early = (X - 1) * half
    terms = [
        (rows_of[:early], [block[place * half : (place + 1) * half] for block in (delta, before, after)])
        for place, rows_of in enumerate((own, other))
    ]
    terms.append((jnp.concatenate([own[early:], other[early:]], axis=0), [across]))
    product = 0.0
    for left, right in terms:
        product += lax.dot_general(
            left,
            jnp.concatenate(right, axis=0),
            (((0,), (0,)), ((), ())),
            preferred_element_type=jnp.float32,
        )

    count = Z // W
    keep, above, across_rows, below = pl.pallas_call(
        slab_kernel,
        out_shape=[shape((count, owned, units), jnp.float32)]
        + [shape((count, owned, units), jnp.bfloat16)] * (W - 1),
        in_specs=[SMEM, VMEM],
        out_specs=[VMEM] * W,
        compiler_params=PARAMS,
        name="slabs",
    )(jnp.stack([z_at % W]), product.reshape(Z, owned, units))

    far = z_apart(across_rows, -2)
    above = z_shift(above, 1)
    below = z_shift(below, -1)
    own_block, *blocks = pl.pallas_call(
        window_kernel,
        out_shape=[shape((owned, units), jnp.float32)]
        + [shape((owned, units), jnp.bfloat16)] * (count - 1),
        in_specs=[SMEM] + [VMEM] * 4,
        out_specs=[VMEM] * count,
        compiler_params=PARAMS,
        name="window",
    )(jnp.stack([z_at // W]), keep, far, above, below)

    total = own_block
    for step in (2, 1, 3):
        total += f32(z_shift(blocks[step - 1], W * step))
    return total * (1.0 / math.sqrt(rows * X * Z * Y * C))


def solution(mesh):
    fine = Mesh(mesh.devices.reshape(X, Z, Y, C), ("x", "z", "y", "c"))
    placed = (P(DP + ET, None), P(DP + ET), P(DP + ET), P(DP, ET), P(DP, ET), P(DP, ET))
    return jax.shard_map(
        shards, mesh=fine, in_specs=placed, out_specs=P(DP, ET), check_vma=False
    )
```

```python
import math

import jax
import jax.numpy as jnp
from jax import lax
from jax.experimental import pallas as pl
from jax.experimental.pallas import tpu as pltpu
from jax.sharding import Mesh, PartitionSpec as P

X, Z, Y, C = 4, 16, 4, 2
W = 4
DP = ("x", "z")
ET = ("y", "c")
VMEM = pl.BlockSpec(memory_space=pltpu.VMEM)
SMEM = pl.BlockSpec(memory_space=pltpu.SMEM)
PARAMS = pltpu.CompilerParams(vmem_limit_bytes=11 * 512 * 1024)


def f32(value):
    return value.astype(jnp.float32)


def bf16(value):
    return value.astype(jnp.bfloat16)


def x_shift(value, step):
    return lax.ppermute(value, "x", [(i, (i + step) % X) for i in range(X)])


def x_forward(value):
    pairs = [(x * C + c, (x + 1 - 2 * c) % X * C + c) for x in range(X) for c in range(C)]
    return lax.ppermute(value, ("x", "c"), pairs)


def z_shift(value, step):
    return lax.ppermute(value, "z", [(i, (i + step) % Z) for i in range(Z)])


def z_apart(value, step):
    pairs = [(z * C + c, (z - step + 2 * step * c) % Z * C + c) for z in range(Z) for c in range(C)]
    return lax.ppermute(value, ("z", "c"), pairs)


def spread_kernel(rows_ref, out_ref):
    for place in range(Y):
        out_ref[place] = rows_ref[...]


def choose_kernel(at, before_ref, after_ref, out_ref):
    @pl.when(at[0] == 0)
    def _():
        out_ref[...] = before_ref[...]

    @pl.when(at[0] != 0)
    def _():
        out_ref[...] = after_ref[...]


def order_kernel(at, rows_ref, out_ref):
    rows = rows_ref.shape[2]
    for place in range(X):
        for y in range(Y):
            start = (place * Y + y) * rows
            out_ref[start : start + rows, :] = rows_ref[y, at[place]]


def slab_kernel(at, total_ref, keep_ref, *sent_refs):
    for j in range(Z // W):
        keep_ref[j] = total_ref[j * W + at[0]]
        for step, sent_ref in enumerate(sent_refs):
            sent_ref[j] = bf16(total_ref[j * W + (at[0] + step + 1) % W])


def window_kernel(at, keep_ref, far_ref, above_ref, below_ref, own_ref, *sent_refs):
    for step, out_ref in enumerate((own_ref,) + sent_refs):
        j = (at[0] + step) % (Z // W)
        value = keep_ref[j] + f32(far_ref[j]) + f32(above_ref[j]) + f32(below_ref[j])
        out_ref[...] = value.astype(out_ref.dtype)


def shards(token_rows, route_weight, live_count, gate_pre, up_pre, hidden_grad):
    rows, features = token_rows.shape
    units = gate_pre.shape[1]
    part = features // X
    owned = part // Z
    core = lax.axis_index("c")
    x_at = lax.axis_index("x")
    z_at = lax.axis_index("z")
    shape = jax.ShapeDtypeStruct

    live_rows = jnp.arange(rows, dtype=jnp.int32) < live_count[0]
    factor = route_weight * f32(live_rows)
    weighted = jnp.stack(
        [
            bf16(f32(token_rows[:, k * part : (k + 1) * part]) * factor[:, None])
            for k in range(X)
        ]
    )
    gate = f32(gate_pre)
    sigmoid_v = jax.nn.sigmoid(gate)
    slope = sigmoid_v * (1.0 + gate * (1.0 - sigmoid_v))
    delta = bf16(f32(hidden_grad) * f32(up_pre) * slope).reshape(Y, C, rows, units)
    delta = [
        lax.dynamic_index_in_dim(delta, place, 1, keepdims=False) for place in (core, 1 - core)
    ]
    delta = jnp.stack(delta).reshape(C * Y * rows, units)

    half = Y * rows
    parts = lax.all_to_all(weighted, "x", 0, 0)
    parts, delta = lax.optimization_barrier((parts, delta))
    before, after = x_shift(delta, 1), x_shift(delta, -1)
    chosen = pl.pallas_call(
        choose_kernel,
        out_shape=shape(delta.shape, delta.dtype),
        in_specs=[SMEM, VMEM, VMEM],
        out_specs=VMEM,
        compiler_params=PARAMS,
        cost_estimate=pl.CostEstimate(flops=int(2.3e+10), bytes_accessed=0, transcendentals=0),
        name="chosen",
    )(jnp.stack([core]), before, after)
    across = x_forward(chosen)
    spread = pl.pallas_call(
        spread_kernel,
        out_shape=shape((Y, X, rows, part), jnp.bfloat16),
        in_specs=[VMEM],
        out_specs=VMEM,
        compiler_params=PARAMS,
        cost_estimate=pl.CostEstimate(flops=int(2.3e+10), bytes_accessed=0, transcendentals=0),
        name="spread",
    )(parts)
    own = lax.all_to_all(spread, "y", 0, 0)

    own = pl.pallas_call(
        order_kernel,
        out_shape=shape((X * half, part), jnp.bfloat16),
        in_specs=[SMEM, VMEM],
        out_specs=VMEM,
        compiler_params=PARAMS,
        cost_estimate=pl.CostEstimate(flops=int(2.3e+10), bytes_accessed=0, transcendentals=0),
        name="ordered_rows",
    )((x_at + jnp.array([0, X - 1, 1, 2])) % X, own)
    other = lax.ppermute(own, "c", [(0, 1), (1, 0)])
    early = (X - 1) * half
    terms = [
        (rows_of[:early], [block[place * half : (place + 1) * half] for block in (delta, before, after)])
        for place, rows_of in enumerate((own, other))
    ]
    terms.append((jnp.concatenate([own[early:], other[early:]], axis=0), [across]))
    product = 0.0
    for left, right in terms:
        product += lax.dot_general(
            left,
            jnp.concatenate(right, axis=0),
            (((0,), (0,)), ((), ())),
            preferred_element_type=jnp.float32,
        )

    count = Z // W
    keep, above, across_rows, below = pl.pallas_call(
        slab_kernel,
        out_shape=[shape((count, owned, units), jnp.float32)]
        + [shape((count, owned, units), jnp.bfloat16)] * (W - 1),
        in_specs=[SMEM, VMEM],
        out_specs=[VMEM] * W,
        compiler_params=PARAMS,
        name="slabs",
    )(jnp.stack([z_at % W]), product.reshape(Z, owned, units))

    far = z_apart(across_rows, -2)
    above = z_shift(above, 1)
    below = z_shift(below, -1)
    own_block, *blocks = pl.pallas_call(
        window_kernel,
        out_shape=[shape((owned, units), jnp.float32)]
        + [shape((owned, units), jnp.bfloat16)] * (count - 1),
        in_specs=[SMEM] + [VMEM] * 4,
        out_specs=[VMEM] * count,
        compiler_params=PARAMS,
        name="window",
    )(jnp.stack([z_at // W]), keep, far, above, below)

    total = own_block
    for step in (2, 1, 3):
        total += f32(z_shift(blocks[step - 1], W * step))
    return total * (1.0 / math.sqrt(rows * X * Z * Y * C))


def solution(mesh):
    fine = Mesh(mesh.devices.reshape(X, Z, Y, C), ("x", "z", "y", "c"))
    placed = (P(DP + ET, None), P(DP + ET), P(DP + ET), P(DP, ET), P(DP, ET), P(DP, ET))
    return jax.shard_map(
        shards, mesh=fine, in_specs=placed, out_specs=P(DP, ET), check_vma=False
    )
```

```python
import math

import jax
import jax.numpy as jnp
from jax import lax
from jax.experimental import pallas as pl
from jax.experimental.pallas import tpu as pltpu
from jax.sharding import Mesh, PartitionSpec as P

X, Z, Y, C = 4, 16, 4, 2
W = 4
DP = ("x", "z")
ET = ("y", "c")
VMEM = pl.BlockSpec(memory_space=pltpu.VMEM)
SMEM = pl.BlockSpec(memory_space=pltpu.SMEM)
PARAMS = pltpu.CompilerParams(vmem_limit_bytes=11 * 512 * 1024)


def f32(value):
    return value.astype(jnp.float32)


def bf16(value):
    return value.astype(jnp.bfloat16)


def x_shift(value, step):
    return lax.ppermute(value, "x", [(i, (i + step) % X) for i in range(X)])


def x_forward(value):
    pairs = [(x * C + c, (x + 1 - 2 * c) % X * C + c) for x in range(X) for c in range(C)]
    return lax.ppermute(value, ("x", "c"), pairs)


def z_shift(value, step):
    return lax.ppermute(value, "z", [(i, (i + step) % Z) for i in range(Z)])


def z_apart(value, step):
    pairs = [(z * C + c, (z - step + 2 * step * c) % Z * C + c) for z in range(Z) for c in range(C)]
    return lax.ppermute(value, ("z", "c"), pairs)


def spread_kernel(rows_ref, out_ref):
    for place in range(Y):
        out_ref[place] = rows_ref[...]


def choose_kernel(at, before_ref, after_ref, out_ref):
    @pl.when(at[0] == 0)
    def _():
        out_ref[...] = before_ref[...]

    @pl.when(at[0] != 0)
    def _():
        out_ref[...] = after_ref[...]


def order_kernel(at, rows_ref, out_ref):
    rows = rows_ref.shape[2]
    for place in range(X):
        for y in range(Y):
            start = (place * Y + y) * rows
            out_ref[start : start + rows, :] = rows_ref[y, at[place]]


def slab_kernel(at, total_ref, keep_ref, *sent_refs):
    for j in range(Z // W):
        keep_ref[j] = total_ref[j * W + at[0]]
        for step, sent_ref in enumerate(sent_refs):
            sent_ref[j] = bf16(total_ref[j * W + (at[0] + step + 1) % W])


def window_kernel(at, keep_ref, far_ref, above_ref, below_ref, own_ref, *sent_refs):
    for step, out_ref in enumerate((own_ref,) + sent_refs):
        j = (at[0] + step) % (Z // W)
        value = keep_ref[j] + f32(far_ref[j]) + f32(above_ref[j]) + f32(below_ref[j])
        out_ref[...] = value.astype(out_ref.dtype)


def shards(token_rows, route_weight, live_count, gate_pre, up_pre, hidden_grad):
    rows, features = token_rows.shape
    units = gate_pre.shape[1]
    part = features // X
    owned = part // Z
    core = lax.axis_index("c")
    x_at = lax.axis_index("x")
    z_at = lax.axis_index("z")
    shape = jax.ShapeDtypeStruct

    live = lax.broadcasted_iota(jnp.int32, (rows, part), 0) < live_count[0]
    factor = jnp.broadcast_to(route_weight[:, None], (rows, part)) * f32(live)
    weighted = jnp.stack(
        [bf16(f32(token_rows[:, k * part : (k + 1) * part]) * factor) for k in range(X)]
    )
    gate = f32(gate_pre)
    sigmoid_v = jax.nn.sigmoid(gate)
    slope = sigmoid_v * (1.0 + gate * (1.0 - sigmoid_v))
    delta = bf16(f32(hidden_grad) * f32(up_pre) * slope).reshape(Y, C, rows, units)
    delta = [
        lax.dynamic_index_in_dim(delta, place, 1, keepdims=False) for place in (core, 1 - core)
    ]
    delta = jnp.stack(delta).reshape(C * Y * rows, units)

    half = Y * rows
    parts = lax.all_to_all(weighted, "x", 0, 0)
    parts, delta = lax.optimization_barrier((parts, delta))
    before, after = x_shift(delta, 1), x_shift(delta, -1)
    chosen = pl.pallas_call(
        choose_kernel,
        out_shape=shape(delta.shape, delta.dtype),
        in_specs=[SMEM, VMEM, VMEM],
        out_specs=VMEM,
        compiler_params=PARAMS,
        cost_estimate=pl.CostEstimate(flops=int(2.3e+10), bytes_accessed=0, transcendentals=0),
        name="chosen",
    )(jnp.stack([core]), before, after)
    across = x_forward(chosen)
    spread = pl.pallas_call(
        spread_kernel,
        out_shape=shape((Y, X, rows, part), jnp.bfloat16),
        in_specs=[VMEM],
        out_specs=VMEM,
        compiler_params=PARAMS,
        cost_estimate=pl.CostEstimate(flops=int(2.3e+10), bytes_accessed=0, transcendentals=0),
        name="spread",
    )(parts)
    own = lax.all_to_all(spread, "y", 0, 0)

    own = pl.pallas_call(
        order_kernel,
        out_shape=shape((X * half, part), jnp.bfloat16),
        in_specs=[SMEM, VMEM],
        out_specs=VMEM,
        compiler_params=PARAMS,
        cost_estimate=pl.CostEstimate(flops=int(2.3e+10), bytes_accessed=0, transcendentals=0),
        name="ordered_rows",
    )((x_at + jnp.array([0, X - 1, 1, 2])) % X, own)
    other = lax.ppermute(own, "c", [(0, 1), (1, 0)])
    early = (X - 1) * half
    terms = [
        (rows_of[:early], [block[place * half : (place + 1) * half] for block in (delta, before, after)])
        for place, rows_of in enumerate((own, other))
    ]
    terms.append((jnp.concatenate([own[early:], other[early:]], axis=0), [across]))
    product = 0.0
    for left, right in terms:
        product += lax.dot_general(
            left,
            jnp.concatenate(right, axis=0),
            (((0,), (0,)), ((), ())),
            preferred_element_type=jnp.float32,
        )

    count = Z // W
    keep, above, across_rows, below = pl.pallas_call(
        slab_kernel,
        out_shape=[shape((count, owned, units), jnp.float32)]
        + [shape((count, owned, units), jnp.bfloat16)] * (W - 1),
        in_specs=[SMEM, VMEM],
        out_specs=[VMEM] * W,
        compiler_params=PARAMS,
        name="slabs",
    )(jnp.stack([z_at % W]), product.reshape(Z, owned, units))

    far = z_apart(across_rows, -2)
    above = z_shift(above, 1)
    below = z_shift(below, -1)
    own_block, *blocks = pl.pallas_call(
        window_kernel,
        out_shape=[shape((owned, units), jnp.float32)]
        + [shape((owned, units), jnp.bfloat16)] * (count - 1),
        in_specs=[SMEM] + [VMEM] * 4,
        out_specs=[VMEM] * count,
        compiler_params=PARAMS,
        name="window",
    )(jnp.stack([z_at // W]), keep, far, above, below)

    total = own_block
    for step in (2, 1, 3):
        total += f32(z_shift(blocks[step - 1], W * step))
    return total * (1.0 / math.sqrt(rows * X * Z * Y * C))


def solution(mesh):
    fine = Mesh(mesh.devices.reshape(X, Z, Y, C), ("x", "z", "y", "c"))
    placed = (P(DP + ET, None), P(DP + ET), P(DP + ET), P(DP, ET), P(DP, ET), P(DP, ET))
    return jax.shard_map(
        shards, mesh=fine, in_specs=placed, out_specs=P(DP, ET), check_vma=False
    )
```
